256 devices in a mesh: dp: 64 (over z, x, core), mp: 4 (over y).
Axes of the slice: x: 4, y: 4, z: 8, core: 2. Of those that a mesh axis runs over, the one named last changes fastest.
Arguments:
- queries: bfloat16 [32768, 2560], P('dp', 'mp'), may hold values from -200 to 200
- keys: bfloat16 [32768, 512], P('dp', 'mp'), may hold values from -6 to 6
- values: bfloat16 [32768, 512], P('dp', 'mp'), may hold values from -6 to 6
- grad_out: bfloat16 [32768, 5120], P('dp', 'mp'), may hold values from -6 to 6
- out_weight: bfloat16 [2560, 5120], P('mp'), may hold values from -0.125 to 0.125
- parents: int32 [128], replicated, may hold values from -1 to 126, as said below
- lengths: int32 [128], replicated, may hold values from 64 to 256
Outputs:
- attended: bfloat16 [32768, 2560], P('dp', 'mp')
- grad_queries: bfloat16 [32768, 2560], P('dp', 'mp')
- grad_keys: bfloat16 [32768, 512], P('dp', 'mp')
- grad_values: bfloat16 [32768, 512], P('dp', 'mp')
The draws below stay inside these ranges and needn't reach their ends.
Inputs may be any that keep to these rules, and one draw needn't show every extreme that they name: Segments 2 i and 2 i + 1 lie on index i of dp. Only segments of even index are parents; every odd segment has a parent; no segment has more than 7 ancestors, and some segment has exactly that many.
All inputs are finite; a program needn't handle non-finite values.
Results may differ from the reference program's by a relative error of at most 0.024.
Values may be sent and summed in bfloat16 or wider, within the bound.
No kernel may reach another device: no remote copies, remote signals or barrier semaphores. Data moves between devices by JAX's collectives and lax.ppermute only.
A program may use at most 128 MiB of HBM per device.

```python
import math
import jax
import jax.numpy as jnp
from jax import lax

MODEL_DIM = 5120
HD = 128
QH = 20
KVH = 4
SEG_LEN = 256
LEVELS = 8
GROUP = 5
NSEG = 128
TOKENS = 32768


def shared_keys(key):
    raw_keys = jnp.clip(jax.random.normal(key, (TOKENS, KVH * HD), jnp.float32), -6.0, 6.0)
    return raw_keys


def draw_keys(key, part):
    return shared_keys(key).astype(jnp.bfloat16)


def draw_queries(key, part):
    limit = 6.0
    key = jax.random.fold_in(key, 7)
    raw_rows = jnp.clip(jax.random.normal(key, (TOKENS, QH * HD), jnp.float32), -6.0, 6.0)
    mixed_rows = raw_rows
    return jnp.clip(mixed_rows, -limit, limit).astype(jnp.bfloat16)


def draw_parents(key, part):
    key = jax.random.fold_in(key, 11)
    devices = NSEG // 2
    depth_span = LEVELS - 1
    key_order, key_pick, key_leaf = jax.random.split(key, 3)
    shuffled = jax.random.permutation(key_order, devices)
    rank_of = jnp.argsort(shuffled)
    inner_depth = rank_of % depth_span
    below_depth = jnp.maximum(inner_depth - 1, 0)
    ranks_below = (devices - below_depth + depth_span - 1) // depth_span
    choose = jax.random.randint(key_pick, (devices,), 0, 1 << 20) % ranks_below
    parent_rank = choose * depth_span + below_depth
    inner_parent = jnp.where(inner_depth > 0, 2 * shuffled[parent_rank], -1)
    leaf_parent = 2 * jax.random.randint(key_leaf, (devices,), 0, devices)
    leaf_parent = leaf_parent.at[shuffled[1]].set(2 * (devices - 1))
    leaf_parent = leaf_parent.at[shuffled[0]].set(2 * shuffled[depth_span - 1])
    return jnp.stack([inner_parent, leaf_parent], axis=1).reshape(NSEG).astype(jnp.int32)


def draw_lengths(key, part):
    key = jax.random.fold_in(key, 13)
    key_draw, key_order = jax.random.split(key)
    drawn_lengths = jax.random.randint(key_draw, (NSEG,), SEG_LEN // 4, SEG_LEN + 1)
    shuffled = jax.random.permutation(key_order, NSEG)
    drawn_lengths = drawn_lengths.at[shuffled[0]].set(SEG_LEN).at[shuffled[1]].set(SEG_LEN // 4)
    return drawn_lengths.astype(jnp.int32)


def level_of(stream_key, dims, cuts, low, largest):
    level = 1.0
    for dim, blocks in cuts:
        steps = jax.random.uniform(jax.random.fold_in(jax.random.fold_in(stream_key, 6), dim), (blocks,), jnp.float32, low / len(cuts), largest / len(cuts))
        level = level * jnp.repeat(jnp.exp(steps), dims[dim] // blocks).reshape((-1,) + (1,) * (len(dims) - 1 - dim))
    return level


def gaussian(stream_key, dims, width, bound, pieces=(), held_as=jnp.bfloat16):
    array = width * jax.random.normal(stream_key, dims, jnp.float32)
    if pieces:
        array = array * level_of(stream_key, dims, pieces, -0.22, 0.18)
    return jnp.clip(array, -bound, bound).astype(held_as)


def setup_inputs(seed: int = 0) -> dict:
    arg_keys = jax.random.split(jax.random.key(seed), 8)
    return {
        "queries": draw_queries(jax.random.fold_in(arg_keys[7], 71), 0),
        "keys": draw_keys(jax.random.fold_in(arg_keys[7], 71), 0),
        "values": gaussian(arg_keys[2], (TOKENS, KVH * HD), 1.0, 6.0, ((0, 64), (1, 4))),
        "grad_out": gaussian(arg_keys[3], (TOKENS, MODEL_DIM), 1.0, 6.0, ((0, 64), (1, 4))),
        "out_weight": gaussian(arg_keys[4], (QH * HD, MODEL_DIM), (QH * HD) ** -0.5, 0.125, ((0, 4),)),
        "parents": draw_parents(jax.random.fold_in(arg_keys[7], 71), 0),
        "lengths": draw_lengths(jax.random.fold_in(arg_keys[7], 71), 0),
    }


def to_bfloat(values_in):
    return lax.optimization_barrier(values_in.astype(jnp.bfloat16))

def ancestor_chain(parents):
    current = jnp.arange(NSEG, dtype=jnp.int32)
    columns = [current]
    for hop_index in range(LEVELS - 1):
        current = jnp.where(current >= 0, parents[jnp.maximum(current, 0)], -1).astype(jnp.int32)
        columns.append(current)
    return jnp.stack(columns, axis=1)

def reference(queries, keys, values, grad_out, out_weight, parents, lengths):
    score_scale = 1.0 / math.sqrt(HD)
    attn_grad = jnp.dot(grad_out, out_weight.T, preferred_element_type=jnp.float32)
    positions = jnp.arange(TOKENS, dtype=jnp.int32) % SEG_LEN
    owners = jnp.arange(TOKENS, dtype=jnp.int32) // SEG_LEN
    live_rows = positions < lengths[owners]
    attn_grad = to_bfloat(jnp.where(live_rows[:, None], attn_grad, 0.0))
    chain_ids = ancestor_chain(parents)
    query_blocks = queries.reshape(NSEG, SEG_LEN, KVH, GROUP, HD)
    key_blocks = keys.reshape(NSEG, SEG_LEN, KVH, HD)
    value_blocks = values.reshape(NSEG, SEG_LEN, KVH, HD)
    grad_blocks = attn_grad.reshape(NSEG, SEG_LEN, KVH, GROUP, HD)
    key_pos = jnp.arange(SEG_LEN, dtype=jnp.int32)
    causal = key_pos[None, :] <= key_pos[:, None]
    first_level = jnp.arange(LEVELS, dtype=jnp.int32) == 0

    def one_segment(segment):
        chain = chain_ids[segment]
        present = chain >= 0
        safe_ids = jnp.maximum(chain, 0).astype(jnp.int32)
        key_rows = key_blocks[safe_ids].astype(jnp.float32).reshape(LEVELS * SEG_LEN, KVH, HD)
        value_rows = value_blocks[safe_ids].astype(jnp.float32).reshape(LEVELS * SEG_LEN, KVH, HD)
        valid_keys = present[:, None] & (key_pos[None, :] < lengths[safe_ids][:, None])
        allowed = valid_keys[None, :, :] & (causal[:, None, :] | ~first_level[None, :, None])
        allowed = allowed.reshape(SEG_LEN, LEVELS * SEG_LEN)
        query_rows = query_blocks[segment].astype(jnp.float32)
        scores = jnp.einsum('tkgd,jkd->kgtj', query_rows, key_rows) * score_scale
        masked = jnp.where(allowed, scores, -1e+30)
        row_max = lax.optimization_barrier(jnp.max(masked, axis=-1, keepdims=True))
        exp_total = lax.optimization_barrier(jnp.sum(jnp.where(allowed, jnp.exp(masked - row_max), 0.0), axis=-1, keepdims=True))
        log_total = row_max + jnp.log(exp_total)
        probabilities = jnp.where(allowed, jnp.exp(masked - log_total), 0.0)
        probabilities_low = to_bfloat(probabilities).astype(jnp.float32)
        attended_full = jnp.einsum('kgtj,jkd->tkgd', probabilities_low, value_rows)
        grad_rows = grad_blocks[segment].astype(jnp.float32)
        inner = lax.optimization_barrier(jnp.sum(grad_rows * attended_full, axis=-1))
        grad_probs = jnp.einsum('tkgd,jkd->kgtj', grad_rows, value_rows)
        grad_scores = to_bfloat(probabilities * (grad_probs - jnp.transpose(inner, (1, 2, 0))[..., None])).astype(jnp.float32)
        grad_query = jnp.einsum('kgtj,jkd->tkgd', grad_scores, key_rows) * score_scale
        key_terms = jnp.einsum('kgtj,tkgd->jkd', grad_scores, query_rows) * score_scale
        value_terms = jnp.einsum('kgtj,tkgd->jkd', probabilities_low, grad_rows)
        both_terms = jnp.stack([key_terms.reshape(LEVELS, SEG_LEN, KVH, HD), value_terms.reshape(LEVELS, SEG_LEN, KVH, HD)], axis=0)
        return (attended_full.astype(jnp.bfloat16), grad_query.astype(jnp.bfloat16), both_terms, safe_ids, present)

    def one_pair(carry, pair):
        first_out = one_segment(2 * pair)
        second_out = one_segment(2 * pair + 1)
        grads_acc = carry
        grads_acc = grads_acc.at[:, 2 * pair].add(first_out[2][:, 0])
        grads_acc = grads_acc.at[:, 2 * pair + 1].add(second_out[2][:, 0])
        remote_ids = jnp.concatenate([first_out[3][1:], second_out[3][1:]])
        remote_here = jnp.concatenate([first_out[4][1:], second_out[4][1:]])
        remote_terms = jnp.concatenate([first_out[2][:, 1:], second_out[2][:, 1:]], axis=1)
        count = remote_ids.shape[0]
        match = (remote_ids[:, None] == remote_ids[None, :]) & remote_here[:, None] & remote_here[None, :]
        summed = jnp.einsum('ij,cjtkd->citkd', match.astype(jnp.float32), remote_terms)
        earlier = jnp.arange(count)[None, :] < jnp.arange(count)[:, None]
        seen = jnp.any(match & earlier, axis=1)
        first_seen = (remote_here & ~seen).astype(jnp.float32)
        rounded = to_bfloat(summed).astype(jnp.float32) * first_seen[None, :, None, None, None]
        grads_acc = grads_acc.at[:, remote_ids].add(rounded)
        stacked = (jnp.stack([first_out[0], second_out[0]]), jnp.stack([first_out[1], second_out[1]]))
        return (grads_acc, stacked)
    zero_grads = jnp.zeros((2, NSEG, SEG_LEN, KVH, HD), jnp.float32)
    carried, stacked = lax.scan(one_pair, zero_grads, jnp.arange(NSEG // 2, dtype=jnp.int32))
    attended, grad_queries = stacked
    return (attended.reshape(TOKENS, QH * HD), grad_queries.reshape(TOKENS, QH * HD), carried[0].reshape(TOKENS, KVH * HD).astype(jnp.bfloat16), carried[1].reshape(TOKENS, KVH * HD).astype(jnp.bfloat16))
```

```python
import functools
import math

import jax
import jax.numpy as jnp
from jax import lax
from jax.experimental import pallas as pl
from jax.experimental.pallas import tpu as pltpu
from jax.sharding import Mesh, PartitionSpec as P

SEG = 256
HOPS = 7
NZ, NX, NC = 8, 4, 2
NEG = -1e30
BF = jnp.bfloat16
F32 = jnp.float32
ANY = pl.BlockSpec(memory_space=pl.ANY)
SMEM = pl.BlockSpec(memory_space=pltpu.SMEM)
VMEM = pl.BlockSpec(memory_space=pltpu.VMEM)
PARAMS = pltpu.CompilerParams(vmem_limit_bytes=52 * 1024 * 1024)


def shift(array, axis, step):
    size = {"z": NZ, "x": NX, "core": NC, "mp": 4}[axis]
    return lax.ppermute(array, axis, [(i, (i + step) % size) for i in range(size)])


def dot(left, right):
    return jnp.dot(left, right, preferred_element_type=F32)


def dot_nt(left, right):
    return lax.dot_general(left, right, (((1,), (1,)), ((), ())), preferred_element_type=F32)


def project_first(info, own, after, before, weight, total, g_buf, w_buf, sems):
    mp = info[3]
    copies = []
    for i, (piece, step) in enumerate(((own, 0), (after, 1), (before, 3))):
        column = pl.multiple_of(lax.rem(mp + step, 4) * own.shape[1], 128)
        copies.append(
            (
                pltpu.make_async_copy(piece, g_buf.at[i], sems.at[i, 0]),
                pltpu.make_async_copy(
                    weight.at[:, pl.ds(column, own.shape[1])], w_buf.at[i], sems.at[i, 1]
                ),
            )
        )
    for pair in copies:
        for copy in pair:
            copy.start()
    for i, pair in enumerate(copies):
        for copy in pair:
            copy.wait()

        @pl.loop(0, total.shape[1] // 128)
        def _(n, i=i):
            cols = pl.ds(pl.multiple_of(n * 128, 128), 128)
            part = dot_nt(g_buf[i], w_buf[i, cols, :])
            if i == 0:
                total[:, cols] = part
            else:
                total[:, cols] += part


def project_last(info, lengths, low, high, weight, partial, out, g_buf, w_buf, sems):
    mp = info[3]
    width = low.shape[1]
    column = pl.multiple_of(lax.rem(mp + 2, 4) * width, 128)
    copies = (
        pltpu.make_async_copy(weight.at[:, pl.ds(column, width)], w_buf, sems.at[0]),
        pltpu.make_async_copy(low, g_buf.at[pl.ds(0, SEG)], sems.at[1]),
        pltpu.make_async_copy(high, g_buf.at[pl.ds(SEG, SEG)], sems.at[2]),
    )
    for copy in copies:
        copy.start()
    for copy in copies:
        copy.wait()
    first = 2 * info[4]
    rows = lax.broadcasted_iota(jnp.int32, (2 * SEG, 128), 0)
    limit = jnp.where(rows < SEG, lengths[first], lengths[first + 1] + SEG)
    live = rows < limit

    @pl.loop(0, out.shape[1] // 128)
    def _(n):
        cols = pl.ds(pl.multiple_of(n * 128, 128), 128)
        full = partial[:, cols] + dot_nt(g_buf[...], w_buf[cols, :])
        out[:, cols] = jnp.where(live, full, 0.0).astype(BF)


def project(info, lengths, grad_out, out_weight):
    rows, width = grad_out.shape
    heads = out_weight.shape[0]
    before = shift(grad_out, "mp", 1)
    after = shift(grad_out, "mp", -1)
    low = shift(after[:SEG], "mp", -1)
    high = shift(before[SEG:], "mp", 1)
    partial = pl.pallas_call(
        project_first,
        out_shape=jax.ShapeDtypeStruct((rows, heads), F32),
        in_specs=[SMEM, ANY, ANY, ANY, ANY],
        out_specs=VMEM,
        scratch_shapes=[
            pltpu.VMEM((3, rows, width), BF),
            pltpu.VMEM((3, heads, width), BF),
            pltpu.SemaphoreType.DMA((3, 2)),
        ],
        compiler_params=PARAMS,
        cost_estimate=pl.CostEstimate(flops=6 * rows * heads * width, bytes_accessed=10_000_000, transcendentals=0),
    )(info, grad_out, after, before, out_weight)
    return pl.pallas_call(
        project_last,
        out_shape=jax.ShapeDtypeStruct((rows, heads), BF),
        in_specs=[SMEM, SMEM, ANY, ANY, ANY, VMEM],
        out_specs=VMEM,
        scratch_shapes=[
            pltpu.VMEM((rows, width), BF),
            pltpu.VMEM((heads, width), BF),
            pltpu.SemaphoreType.DMA((3,)),
        ],
        compiler_params=PARAMS,
        cost_estimate=pl.CostEstimate(flops=2 * rows * heads * width, bytes_accessed=6_000_000, transcendentals=0),
    )(info, lengths, low, high, out_weight, partial)


def gather(block):
    line = jnp.stack(
        [block, shift(block, "x", -1), shift(block, "x", 2), shift(block, "x", 1)]
    )
    ahead = [line]
    back = [line]
    for _ in range(3):
        ahead.append(shift(ahead[-1], "z", -1))
        back.append(shift(back[-1], "z", 1))
    far_low = shift(ahead[3][:2], "z", -1)
    far_high = shift(back[3][2:], "z", 1)
    pieces = [line, ahead[1], ahead[2], ahead[3], far_low, far_high, back[3], back[2], back[1]]
    return pieces, [shift(piece, "core", 1) for piece in pieces]


def for_piece(dz, dx, action):
    for k in range(4):
        pl.when(dz == k)(functools.partial(action, k, dx))
    pl.when((dz == 4) & (dx < 2))(functools.partial(action, 4, dx))
    pl.when((dz == 4) & (dx >= 2))(functools.partial(action, 5, dx - 2))
    for k in range(5, 8):
        pl.when(dz == k)(functools.partial(action, k + 1, dx))


def place(info, ancestor):
    owner = lax.div(ancestor, 2)
    dz = lax.rem(lax.div(owner, NX * NC) - info[0] + NZ, NZ)
    dx = lax.rem(lax.rem(lax.div(owner, NC), NX) - info[1] + NX, NX)
    return dz, dx, lax.rem(owner, NC) == info[2]


def attention(info, parents, lengths, q, do, ko, vo, *refs):
    near = refs[:9]
    other = refs[9:18]
    att_out, dq_out, own_out, slots = refs[18:22]
    (kv, p_buf, kt_buf, q_st, q_t, do_st, do_t, att, dq_t, m_ref, l_ref, m_lev, f_buf,
     p_low, ds_buf, lens, sems) = refs[22:]
    group = q.shape[1] // 128
    width = group * SEG
    scale = 1.0 / math.sqrt(128)
    coef = scale * math.log2(math.e)
    first = 2 * info[4]

    depths = []
    for s in range(2):

        def hop(i, carry, s=s):
            current, depth = carry
            current = jnp.where(current >= 0, parents[jnp.maximum(current, 0)], -1)
            slot = s * HOPS + i

            @pl.when(current >= 0)
            def _():
                lens[slot] = lengths[current]
                dz, dx, same = place(info, current)

                def start(source, k, b):
                    pltpu.make_async_copy(source[k].at[b], kv.at[slot], sems.at[slot]).start()

                @pl.when(same)
                def _():
                    for_piece(dz, dx, functools.partial(start, near))

                @pl.when(jnp.logical_not(same))
                def _():
                    for_piece(dz, dx, functools.partial(start, other))

            return current, depth + (current >= 0).astype(jnp.int32)

        depths.append(lax.fori_loop(0, HOPS, hop, (first + s, jnp.int32(0)))[1])

    key_row = lax.broadcasted_iota(jnp.int32, (SEG, SEG), 0)
    query_row = lax.broadcasted_iota(jnp.int32, (SEG, SEG), 1)
    spans = [slice(h * SEG, (h + 1) * SEG) for h in range(group)]

    def forward(level, k, v, allowed, start):
        v_t = v.T
        kt_buf[level] = k.T
        for span in spans:
            s = jnp.where(allowed, dot(k, q_t[:, span]), NEG)
            top = jnp.max(s, axis=0, keepdims=True)
            if not start:
                old = m_ref[:, span]
                top = jnp.maximum(top, old)
                alpha = jnp.exp2((old - top) * coef)
            p = jnp.exp2((s - top) * coef)
            total = jnp.sum(p, axis=0, keepdims=True)
            p = p.astype(BF)
            p_buf[level, :, span] = p
            part = dot(v_t, p)
            m_ref[:, span] = top
            m_lev[level, :, span] = top
            if start:
                l_ref[:, span] = total
                att[:, span] = part
            else:
                l_ref[:, span] = l_ref[:, span] * alpha + total
                att[:, span] = att[:, span] * alpha + part

    def backward(level, k, v, start):
        k_t = kt_buf[level]
        for span in spans:
            weight = jnp.exp2((m_lev[level, :, span] - m_ref[:, span]) * coef) * l_ref[:, span]
            p = p_buf[level, :, span].astype(F32) * weight
            p_low[:, span] = p.astype(BF)
            ds = (p * (dot(v, do_t[:, span]) - f_buf[:, span])).astype(BF)
            ds_buf[:, span] = ds
            part = dot(k_t, ds)
            if start:
                dq_t[:, span] = part
            else:
                dq_t[:, span] += part
        return dot(ds_buf[...], q_st[...]) * scale, dot(p_low[...], do_st[...])

    for s in range(2):
        rows = slice(s * SEG, (s + 1) * SEG)
        depth = depths[s]
        for h, span in enumerate(spans):
            cols = slice(h * 128, (h + 1) * 128)
            q_st[span, :] = q[rows, cols]
            q_t[:, span] = q[rows, cols].T
            do_st[span, :] = do[rows, cols]
            do_t[:, span] = do[rows, cols].T
        k = ko[rows, :]
        v = vo[rows, :]
        forward(0, k, v, (key_row <= query_row) & (key_row < lengths[first + s]), True)

        def forward_step(i, _, s=s):
            slot = s * HOPS + i
            pltpu.make_async_copy(near[0].at[0], kv.at[slot], sems.at[slot]).wait()
            forward(i + 1, kv[slot, :, :128], kv[slot, :, 128:], key_row < lens[slot], False)
            return 0

        lax.fori_loop(0, depth, forward_step, 0)
        for h, span in enumerate(spans):
            cols = slice(h * 128, (h + 1) * 128)
            inverse = 1.0 / l_ref[:, span]
            l_ref[:, span] = inverse
            full = att[:, span] * inverse
            f_buf[:, span] = jnp.sum(full * do_t[:, span].astype(F32), axis=0, keepdims=True)
            att_out[rows, cols] = full.T.astype(BF)
        dk, dv = backward(0, k, v, True)
        own_out[rows, :128] = dk
        own_out[rows, 128:] = dv

        def backward_step(i, _, s=s):
            slot = s * HOPS + i
            dk, dv = backward(i + 1, kv[slot, :, :128], kv[slot, :, 128:], False)
            slots[slot, :, :128] = dk.astype(BF)
            slots[slot, :, 128:] = dv.astype(BF)
            return 0

        lax.fori_loop(0, depth, backward_step, 0)
        for h, span in enumerate(spans):
            cols = slice(h * 128, (h + 1) * 128)
            dq_out[rows, cols] = (dq_t[:, span] * scale).T.astype(BF)


def attend(info, parents, lengths, q, do, ko, vo, near, other):
    rows, features = q.shape
    width = features // 128 * SEG
    return pl.pallas_call(
        attention,
        out_shape=(
            jax.ShapeDtypeStruct((rows, features), BF),
            jax.ShapeDtypeStruct((rows, features), BF),
            jax.ShapeDtypeStruct((rows, 256), F32),
            jax.ShapeDtypeStruct((2 * HOPS, SEG, 256), BF),
        ),
        in_specs=[SMEM, SMEM, SMEM, VMEM, VMEM, VMEM, VMEM] + [ANY] * 18,
        out_specs=(VMEM,) * 4,
        scratch_shapes=[
            pltpu.VMEM((2 * HOPS, SEG, 256), BF),
            pltpu.VMEM((HOPS + 1, SEG, width), BF),
            pltpu.VMEM((HOPS + 1, 128, SEG), BF),
            pltpu.VMEM((width, 128), BF),
            pltpu.VMEM((128, width), BF),
            pltpu.VMEM((width, 128), BF),
            pltpu.VMEM((128, width), BF),
            pltpu.VMEM((128, width), F32),
            pltpu.VMEM((128, width), F32),
            pltpu.VMEM((1, width), F32),
            pltpu.VMEM((1, width), F32),
            pltpu.VMEM((HOPS + 1, 1, width), F32),
            pltpu.VMEM((1, width), F32),
            pltpu.VMEM((SEG, width), BF),
            pltpu.VMEM((SEG, width), BF),
            pltpu.SMEM((2 * HOPS,), jnp.int32),
            pltpu.SemaphoreType.DMA((2 * HOPS,)),
        ],
        compiler_params=PARAMS,
        cost_estimate=pl.CostEstimate(flops=8_000_000_000, bytes_accessed=8_000_000, transcendentals=5_000_000),
    )(info, parents, lengths, q, do, ko, vo, *near, *other)


def combine_kernel(info, parents, mine, theirs, *outs):
    for out in outs:
        out[...] = jnp.zeros(out.shape, BF)
    for source, device in ((mine, info[4]), (theirs, info[4] + 1 - 2 * info[2])):
        for s in range(2):

            def hop(i, current, source=source, device=device, s=s):
                current = jnp.where(current >= 0, parents[jnp.maximum(current, 0)], -1)
                dz, dx, same = place(info, current)

                @pl.when((current >= 0) & same)
                def _():
                    def add(k, b):
                        outs[k][b] = (outs[k][b].astype(F32) + source[s * HOPS + i].astype(F32)).astype(BF)

                    for_piece(dz, dx, add)

                return current

            lax.fori_loop(0, HOPS, hop, 2 * device + s)


def scatter(info, parents, mine):
    theirs = shift(mine, "core", 1)
    counts = (4, 4, 4, 4, 2, 2, 4, 4, 4)
    sums = pl.pallas_call(
        combine_kernel,
        out_shape=tuple(jax.ShapeDtypeStruct((n, SEG, 256), BF) for n in counts),
        in_specs=[SMEM, SMEM, VMEM, VMEM],
        out_specs=(VMEM,) * 9,
        compiler_params=PARAMS,
        cost_estimate=pl.CostEstimate(flops=10_000_000, bytes_accessed=8_000_000, transcendentals=0),
    )(info, parents, mine, theirs)

    def plus(a, b):
        return (a.astype(F32) + b.astype(F32)).astype(BF)

    up = shift(sums[4], "z", 1)
    down = shift(sums[5], "z", -1)
    up = jnp.concatenate([plus(sums[3][:2], up), sums[3][2:]])
    down = jnp.concatenate([sums[6][:2], plus(sums[6][2:], down)])
    for a, b in ((2, 7), (1, 8)):
        up = plus(sums[a], shift(up, "z", 1))
        down = plus(sums[b], shift(down, "z", -1))
    up = shift(up, "z", 1)
    down = shift(down, "z", -1)
    line = (sums[0].astype(F32) + up.astype(F32) + down.astype(F32)).astype(BF)
    return (
        line[0].astype(F32)
        + shift(line[1], "x", 1).astype(F32)
        + shift(line[2], "x", 2).astype(F32)
        + shift(line[3], "x", -1).astype(F32)
    )


def body(queries, keys, values, grad_out, out_weight, parents, lengths):
    z = lax.axis_index("z")
    x = lax.axis_index("x")
    core = lax.axis_index("core")
    info = jnp.stack([z, x, core, lax.axis_index("mp"), (z * NX + x) * NC + core]).astype(jnp.int32)
    block = jnp.concatenate([keys[:SEG], values[:SEG]], axis=1)
    near, other = gather(block)
    attn_grad = project(info, lengths, grad_out, out_weight)
    attended, grad_queries, own, slots = attend(
        info, parents, lengths, queries, attn_grad, keys, values, near, other
    )
    remote = scatter(info, parents, slots)
    gradients = jnp.concatenate([own[:SEG] + remote, own[SEG:]])
    return (
        attended,
        grad_queries,
        gradients[:, :128].astype(BF),
        gradients[:, 128:].astype(BF),
    )


def solution(mesh):
    fine = Mesh(mesh.devices.reshape(NZ, NX, NC, 4), ("z", "x", "core", "mp"))
    rows = ("z", "x", "core")
    return jax.shard_map(
        body,
        mesh=fine,
        in_specs=(P(rows, "mp"),) * 4 + (P("mp", None), P(), P()),
        out_specs=(P(rows, "mp"),) * 4,
        check_vma=False,
    )
```

```python
import functools
import math

import jax
import jax.numpy as jnp
from jax import lax
from jax.experimental import pallas as pl
from jax.experimental.pallas import tpu as pltpu
from jax.sharding import Mesh, PartitionSpec as P

SEG = 256
HOPS = 7
ROWS = HOPS * SEG + 2 * SEG
NZ, NX, NC = 8, 4, 2
NEG = -1e30
BF = jnp.bfloat16
F32 = jnp.float32
ANY = pl.BlockSpec(memory_space=pl.ANY)
SMEM = pl.BlockSpec(memory_space=pltpu.SMEM)
VMEM = pl.BlockSpec(memory_space=pltpu.VMEM)
PARAMS = pltpu.CompilerParams(vmem_limit_bytes=52 * 1024 * 1024)


def shift(array, axis, step):
    size = {"z": NZ, "x": NX, "core": NC, "mp": 4}[axis]
    return lax.ppermute(array, axis, [(i, (i + step) % size) for i in range(size)])


def dot(left, right):
    return jnp.dot(left, right, preferred_element_type=F32)


def dot_nt(left, right):
    return lax.dot_general(left, right, (((1,), (1,)), ((), ())), preferred_element_type=F32)


def project_first(info, own, after, before, weight, total, g_buf, w_buf, sems):
    mp = info[3]
    copies = []
    for i, (piece, step) in enumerate(((own, 0), (after, 1), (before, 3))):
        column = pl.multiple_of(lax.rem(mp + step, 4) * own.shape[1], 128)
        copies.append(
            (
                pltpu.make_async_copy(piece, g_buf.at[i], sems.at[i, 0]),
                pltpu.make_async_copy(
                    weight.at[:, pl.ds(column, own.shape[1])], w_buf.at[i], sems.at[i, 1]
                ),
            )
        )
    for pair in copies:
        for copy in pair:
            copy.start()
    for i, pair in enumerate(copies):
        for copy in pair:
            copy.wait()

        part = dot_nt(g_buf[i], w_buf[i])
        if i == 0:
            total[...] = part
        else:
            total[...] += part


def project_last(info, lengths, low, high, weight, partial, out, g_buf, w_buf, sems):
    mp = info[3]
    width = low.shape[1]
    column = pl.multiple_of(lax.rem(mp + 2, 4) * width, 128)
    copies = (
        pltpu.make_async_copy(weight.at[:, pl.ds(column, width)], w_buf, sems.at[0]),
        pltpu.make_async_copy(low, g_buf.at[pl.ds(0, SEG)], sems.at[1]),
        pltpu.make_async_copy(high, g_buf.at[pl.ds(SEG, SEG)], sems.at[2]),
    )
    for copy in copies:
        copy.start()
    for copy in copies:
        copy.wait()
    first = 2 * info[4]
    rows = lax.broadcasted_iota(jnp.int32, out.shape, 0)
    limit = jnp.where(rows < SEG, lengths[first], lengths[first + 1] + SEG)
    live = rows < limit

    full = partial[...] + dot_nt(g_buf[...], w_buf[...])
    out[...] = jnp.where(live, full, 0.0).astype(BF)


def project_begin(info, grad_out, after, before, out_weight, *later_than):
    rows, width = grad_out.shape
    heads = out_weight.shape[0]
    return pl.pallas_call(
        lambda info, own, after, before, weight, *rest: project_first(
            info, own, after, before, weight, *rest[len(later_than) :]
        ),
        out_shape=jax.ShapeDtypeStruct((rows, heads), F32),
        in_specs=[SMEM] + [ANY] * (4 + len(later_than)),
        out_specs=VMEM,
        scratch_shapes=[
            pltpu.VMEM((3, rows, width), BF),
            pltpu.VMEM((3, heads, width), BF),
            pltpu.SemaphoreType.DMA((3, 2)),
        ],
        compiler_params=PARAMS,
        cost_estimate=pl.CostEstimate(flops=6 * rows * heads * width, bytes_accessed=10_000_000, transcendentals=0),
    )(info, grad_out, after, before, out_weight, *later_than)


def project_end(info, lengths, low, high, out_weight, partial):
    rows, heads = partial.shape
    width = low.shape[1]
    return pl.pallas_call(
        project_last,
        out_shape=jax.ShapeDtypeStruct((rows, heads), BF),
        in_specs=[SMEM, SMEM, ANY, ANY, ANY, VMEM],
        out_specs=VMEM,
        scratch_shapes=[
            pltpu.VMEM((rows, width), BF),
            pltpu.VMEM((heads, width), BF),
            pltpu.SemaphoreType.DMA((3,)),
        ],
        compiler_params=PARAMS,
        cost_estimate=pl.CostEstimate(flops=2 * rows * heads * width, bytes_accessed=6_000_000, transcendentals=0),
    )(info, lengths, low, high, out_weight, partial)


def cut_kernel(ahead, back, _, low, high):
    low[...] = ahead[...]
    high[...] = back[...]


def cut(ahead, back, later_than):
    shape = (ahead.shape[0] // 2,) + ahead.shape[1:]
    half = jax.ShapeDtypeStruct(shape, ahead.dtype)
    return pl.pallas_call(
        cut_kernel,
        grid=(1,),
        out_shape=(half, half),
        in_specs=[
            pl.BlockSpec(shape, lambda i: (0, 0, 0)),
            pl.BlockSpec(shape, lambda i: (1, 0, 0)),
            ANY,
        ],
        out_specs=(pl.BlockSpec(shape, lambda i: (0, 0, 0)),) * 2,
        compiler_params=PARAMS,
        cost_estimate=pl.CostEstimate(flops=0, bytes_accessed=1_000_000, transcendentals=0),
    )(ahead, back, later_than)


def gather(info, lengths, block, grad_out, out_weight):
    before = shift(grad_out, "mp", 1)
    after = shift(grad_out, "mp", -1)
    line = jnp.stack(
        [block, shift(block, "x", -1), shift(block, "x", 2), shift(block, "x", 1)]
    )
    ahead = [line]
    back = [line]
    for _ in range(3):
        ahead.append(shift(ahead[-1], "z", -1))
        back.append(shift(back[-1], "z", 1))
    low = shift(after[:SEG], "mp", -1)
    high = shift(before[SEG:], "mp", 1)
    partial = project_begin(info, grad_out, after, before, out_weight, ahead[2], back[2])
    far_low, far_high = cut(ahead[3], back[3], partial)
    far_low = shift(far_low, "z", -1)
    far_high = shift(far_high, "z", 1)
    pieces = [line, ahead[1], ahead[2], ahead[3], far_low, far_high, back[3], back[2], back[1]]
    pieces += [shift(piece, "core", 1) for piece in pieces]
    return pieces, project_end(info, lengths, low, high, out_weight, partial)


def for_piece(dz, dx, action):
    for k in range(4):
        pl.when(dz == k)(functools.partial(action, k, dx))
    pl.when((dz == 4) & (dx < 2))(functools.partial(action, 4, dx))
    pl.when((dz == 4) & (dx >= 2))(functools.partial(action, 5, dx - 2))
    for k in range(5, 8):
        pl.when(dz == k)(functools.partial(action, k + 1, dx))


def place(info, ancestor):
    owner = lax.div(ancestor, 2)
    dz = lax.rem(lax.div(owner, NX * NC) - info[0] + NZ, NZ)
    dx = lax.rem(lax.rem(lax.div(owner, NC), NX) - info[1] + NX, NX)
    return dz, dx, lax.rem(owner, NC) == info[2]


def start_fetch(info, parents, lengths, near, other, kv, lens, sems):
    depths = []
    for s in range(2):

        def hop(i, carry, s=s):
            current, depth = carry
            current = jnp.where(current >= 0, parents[jnp.maximum(current, 0)], -1)
            slot = s * HOPS + i

            @pl.when(current >= 0)
            def _():
                lens[slot] = lengths[current]
                dz, dx, same = place(info, current)

                def start(source, k, b):
                    pltpu.make_async_copy(source[k].at[b], kv.at[slot], sems.at[slot]).start()

                @pl.when(same)
                def _():
                    for_piece(dz, dx, functools.partial(start, near))

                @pl.when(jnp.logical_not(same))
                def _():
                    for_piece(dz, dx, functools.partial(start, other))

            return current, depth + (current >= 0).astype(jnp.int32)

        depths.append(lax.fori_loop(0, HOPS, hop, (2 * info[4] + s, jnp.int32(0)))[1])
    return depths


def wait_fetch(near, kv, sems, slot):
    pltpu.make_async_copy(near[0].at[0], kv.at[slot], sems.at[slot]).wait()


def pack(slot, depth, near, kv, lens, starts, sems, store):
    def one(i, row):
        wait_fetch(near, kv, sems, slot + i)
        starts[slot + i] = row
        store(row, kv[slot + i, :, :128], kv[slot + i, :, 128:], lens[slot + i])
        return row + (lens[slot + i] + 15) // 16 * 16

    total = lax.fori_loop(0, depth, one, jnp.int32(0))
    none = jnp.zeros((SEG, 128), BF)
    for i in range(2):
        store(total + i * SEG, none, none, 0)
    return total


def rows_at(row, count):
    return pl.ds(pl.multiple_of(row, 16), count)


def for_rows(total, step):
    def whole(i, _):
        step(512 * i, 512)
        return 0

    count = (total + 255) // 512
    lax.fori_loop(0, count, whole, 0)
    rest = total - 512 * count
    pl.when((rest > 0) & (rest <= 128))(lambda: step(512 * count, 128))
    pl.when(rest > 128)(lambda: step(512 * count, 256))


def widen(block, length):
    row = lax.broadcasted_iota(jnp.int32, block.shape, 0)
    col = lax.broadcasted_iota(jnp.int32, block.shape, 1)
    bias = jnp.where(row < length, 0.0, NEG)
    extra = jnp.where(col == 0, bias, jnp.where(col < 4, 1.0, 0.0))
    return jnp.concatenate([block, extra.astype(BF)], axis=1)


def split_rows(lead, value):
    high = value.astype(BF).astype(F32)
    mid = (value - high).astype(BF).astype(F32)
    low = value - high - mid
    shape = (128, value.shape[1])
    row = lax.broadcasted_iota(jnp.int32, shape, 0)
    out = jnp.where(row == 0, lead, 0.0)
    for i, part in enumerate((high, mid, low)):
        out = jnp.where(row == i + 1, jnp.broadcast_to(part, shape), out)
    return out.astype(BF)


def head_spans(width):
    return [slice(h * SEG, (h + 1) * SEG) for h in range(width // SEG)]


def own_mask(length):
    key_row = lax.broadcasted_iota(jnp.int32, (SEG, SEG), 0)
    query_row = lax.broadcasted_iota(jnp.int32, (SEG, SEG), 1)
    return (key_row <= query_row) & (key_row < length)


def forward_kernel(info, parents, lengths, q, ko, vo, *refs):
    near, other = refs[:9], refs[9:18]
    att_out, full_out, lse_out = refs[18:21]
    kv, k_rows, v_rows, q_t, m_ref, l_ref, lens, starts, sems = refs[21:]
    width = q_t.shape[1]
    coef = math.log2(math.e) / math.sqrt(128)
    first = 2 * info[4]
    spans = head_spans(width)
    depths = start_fetch(info, parents, lengths, near, other, kv, lens, sems)

    for s in range(2):
        rows = slice(s * SEG, (s + 1) * SEG)
        att = full_out.at[s]
        q_t[128:, :] = split_rows(1.0, jnp.zeros((1, width), F32))
        for h, span in enumerate(spans):
            q_t[:128, span] = q[rows, h * 128 : (h + 1) * 128].T

        def update(blocks, mask=None, s=s, att=att):
            v_t = jnp.concatenate([v.T for _, v in blocks], axis=1)
            scores = [[dot(k, q_t[:, span]) for k, _ in blocks] for span in spans]
            if mask is None:
                old = [m_ref[:, span] for span in spans]
                old_l = [l_ref[:, span] for span in spans]
            tops, probs, totals, scales = [], [], [], []
            for h, group in enumerate(scores):
                if mask is not None:
                    group = [jnp.where(mask, group[0], NEG)]
                top = functools.reduce(
                    jnp.maximum, [jnp.max(x, axis=0, keepdims=True) for x in group]
                )
                if mask is None:
                    top = jnp.maximum(top, old[h])
                    scales.append(jnp.exp2((old[h] - top) * coef))
                p = [jnp.exp2((x - top) * coef) for x in group]
                totals.append(sum(jnp.sum(x, axis=0, keepdims=True) for x in p))
                tops.append(top)
                probs.append(jnp.concatenate([x.astype(BF) for x in p], axis=0))
            parts = [dot(v_t, p) for p in probs]
            for h, span in enumerate(spans):
                m_ref[:, span] = tops[h]
                if mask is None:
                    l_ref[:, span] = old_l[h] * scales[h] + totals[h]
                    att[:, span] = att[:, span] * scales[h] + parts[h]
                else:
                    l_ref[:, span] = totals[h]
                    att[:, span] = parts[h]

        length = lengths[first + s]
        update([(widen(ko[rows, :], length), vo[rows, :])], own_mask(length))

        def store(row, k, v, used):
            k_rows[rows_at(row, SEG), :] = widen(k, used)
            v_rows[rows_at(row, SEG), :] = v

        def step(row, count, update=update):
            here = rows_at(row, count)
            update([(k_rows[here, :], v_rows[here, :])])

        for_rows(pack(s * HOPS, depths[s], near, kv, lens, starts, sems, store), step)
        for h, span in enumerate(spans):
            total = l_ref[:, span]
            full = att[:, span] * (1.0 / total)
            att[:, span] = full
            lse_out[s, :, span] = m_ref[:, span] + jnp.log2(total) * (1.0 / coef)
            att_out[rows, h * 128 : (h + 1) * 128] = full.T.astype(BF)


def backward_kernel(info, parents, lengths, q, do, ko, vo, full, lse, *refs):
    near, other = refs[:9], refs[9:18]
    dq_out, own_out, slots = refs[18:21]
    kv, k_rows, v_rows, dk_rows, dv_rows, q_t, q_st, do_t, do_st, dq_t, lens, starts, sems = refs[21:]
    width = q_t.shape[1]
    scale = 1.0 / math.sqrt(128)
    coef = math.log2(math.e) / math.sqrt(128)
    first = 2 * info[4]
    spans = head_spans(width)
    depths = start_fetch(info, parents, lengths, near, other, kv, lens, sems)

    for s in range(2):
        rows = slice(s * SEG, (s + 1) * SEG)
        for h, span in enumerate(spans):
            cols = slice(h * 128, (h + 1) * 128)
            q_st[span, :] = q[rows, cols]
            q_t[:128, span] = q[rows, cols].T
            do_st[span, :] = do[rows, cols]
            turned = do[rows, cols].T
            do_t[:128, span] = turned
            inner = jnp.sum(turned.astype(F32) * full[s, :, span], axis=0, keepdims=True)
            q_t[128:, span] = split_rows(1.0, -lse[s, :, span])
            do_t[128:, span] = split_rows(0.0, -inner)

        def update(blocks, mask=None):
            k_t = jnp.concatenate([k[:, :128].T for k, _ in blocks], axis=1)
            keys = [k for k, _ in blocks]
            vals = [v for _, v in blocks]
            scores = [[dot(k, q_t[:, span]) for k in keys] for span in spans]
            grads = [[dot(v, do_t[:, span]) for v in vals] for span in spans]
            probs = [[] for _ in blocks]
            steps = [[] for _ in blocks]
            for h in range(len(spans)):
                for j in range(len(blocks)):
                    x = scores[h][j]
                    if mask is not None:
                        x = jnp.where(mask, x, NEG)
                    p = jnp.exp2(x * coef)
                    probs[j].append(p.astype(BF))
                    steps[j].append((p * grads[h][j]).astype(BF))
            for h, span in enumerate(spans):
                part = dot(k_t, jnp.concatenate([d[h] for d in steps], axis=0))
                if mask is None:
                    dq_t[:, span] += part
                else:
                    dq_t[:, span] = part
            return [
                (
                    dot(jnp.concatenate(steps[j], axis=1), q_st[...]) * scale,
                    dot(jnp.concatenate(probs[j], axis=1), do_st[...]),
                )
                for j in range(len(blocks))
            ]

        length = lengths[first + s]
        ((dk, dv),) = update([(widen(ko[rows, :], length), widen(vo[rows, :], length))], own_mask(length))
        own_out[rows, :128] = dk
        own_out[rows, 128:] = dv

        def store(row, k, v, used):
            k_rows[rows_at(row, SEG), :] = widen(k, used)
            v_rows[rows_at(row, SEG), :] = widen(v, used)

        def step(row, count, update=update):
            here = rows_at(row, count)
            ((dk, dv),) = update([(k_rows[here, :], v_rows[here, :])])
            dk_rows[here, :] = dk.astype(BF)
            dv_rows[here, :] = dv.astype(BF)

        for_rows(pack(s * HOPS, depths[s], near, kv, lens, starts, sems, store), step)

        def unpack(i, _, s=s):
            slot = s * HOPS + i
            here = rows_at(starts[slot], SEG)
            used = lax.broadcasted_iota(jnp.int32, (SEG, 128), 0) < lens[slot]
            zero = jnp.zeros((SEG, 128), BF)
            slots[slot, :, :128] = jnp.where(used, dk_rows[here, :], zero)
            slots[slot, :, 128:] = jnp.where(used, dv_rows[here, :], zero)
            return 0

        lax.fori_loop(0, depths[s], unpack, 0)
        for h, span in enumerate(spans):
            dq_out[rows, h * 128 : (h + 1) * 128] = (dq_t[:, span] * scale).T.astype(BF)


def attend_forward(info, parents, lengths, q, ko, vo, near, other):
    rows, features = q.shape
    width = features // 128 * SEG
    return pl.pallas_call(
        forward_kernel,
        out_shape=(
            jax.ShapeDtypeStruct((rows, features), BF),
            jax.ShapeDtypeStruct((2, 128, width), F32),
            jax.ShapeDtypeStruct((2, 1, width), F32),
        ),
        in_specs=[SMEM, SMEM, SMEM, VMEM, VMEM, VMEM] + [ANY] * 18,
        out_specs=(VMEM,) * 3,
        scratch_shapes=[
            pltpu.VMEM((2 * HOPS, SEG, 256), BF),
            pltpu.VMEM((ROWS, 256), BF),
            pltpu.VMEM((ROWS, 128), BF),
            pltpu.VMEM((256, width), BF),
            pltpu.VMEM((1, width), F32),
            pltpu.VMEM((1, width), F32),
            pltpu.SMEM((2 * HOPS,), jnp.int32),
            pltpu.SMEM((2 * HOPS,), jnp.int32),
            pltpu.SemaphoreType.DMA((2 * HOPS,)),
        ],
        compiler_params=PARAMS,
        cost_estimate=pl.CostEstimate(flops=3_000_000_000, bytes_accessed=8_000_000, transcendentals=5_000_000),
    )(info, parents, lengths, q, ko, vo, *near, *other)


def attend_backward(info, parents, lengths, q, do, ko, vo, full, lse, near, other):
    rows, features = q.shape
    width = features // 128 * SEG
    return pl.pallas_call(
        backward_kernel,
        out_shape=(
            jax.ShapeDtypeStruct((rows, features), BF),
            jax.ShapeDtypeStruct((rows, 256), F32),
            jax.ShapeDtypeStruct((2 * HOPS, SEG, 256), BF),
        ),
        in_specs=[SMEM, SMEM, SMEM] + [VMEM] * 6 + [ANY] * 18,
        out_specs=(VMEM,) * 3,
        scratch_shapes=[
            pltpu.VMEM((2 * HOPS, SEG, 256), BF),
            pltpu.VMEM((ROWS, 256), BF),
            pltpu.VMEM((ROWS, 256), BF),
            pltpu.VMEM((ROWS, 128), BF),
            pltpu.VMEM((ROWS, 128), BF),
            pltpu.VMEM((256, width), BF),
            pltpu.VMEM((width, 128), BF),
            pltpu.VMEM((256, width), BF),
            pltpu.VMEM((width, 128), BF),
            pltpu.VMEM((128, width), F32),
            pltpu.SMEM((2 * HOPS,), jnp.int32),
            pltpu.SMEM((2 * HOPS,), jnp.int32),
            pltpu.SemaphoreType.DMA((2 * HOPS,)),
        ],
        compiler_params=PARAMS,
        cost_estimate=pl.CostEstimate(flops=8_000_000_000, bytes_accessed=8_000_000, transcendentals=5_000_000),
    )(info, parents, lengths, q, do, ko, vo, full, lse, *near, *other)


COUNTS = (NX,) * 4 + (NX // 2,) * 2 + (NX,) * 3
FIRST = (4, 5)
REST = (3, 6, 2, 7, 1, 8, 0)


def combine_kernel(chunks, info, parents, mine, theirs, *refs):
    outs = dict(zip(chunks, refs[-len(chunks) :]))
    for out in outs.values():
        out[...] = jnp.zeros(out.shape, BF)
    for source, device in ((mine, info[4]), (theirs, info[4] + 1 - 2 * info[2])):
        for s in range(2):

            def hop(i, current, source=source, device=device, s=s):
                current = jnp.where(current >= 0, parents[jnp.maximum(current, 0)], -1)
                dz, dx, same = place(info, current)

                @pl.when((current >= 0) & same)
                def _():
                    def add(k, b):
                        if k in outs:
                            out = outs[k]
                            term = source[s * HOPS + i].astype(F32)
                            out[b] = (out[b].astype(F32) + term).astype(BF)

                    for_piece(dz, dx, add)

                return current

            lax.fori_loop(0, HOPS, hop, 2 * device + s)


def combine(chunks, info, parents, mine, theirs, *later_than):
    return pl.pallas_call(
        functools.partial(combine_kernel, chunks),
        out_shape=tuple(jax.ShapeDtypeStruct((COUNTS[k], SEG, 256), BF) for k in chunks),
        in_specs=[SMEM, SMEM, VMEM, VMEM] + [ANY] * len(later_than),
        out_specs=(VMEM,) * len(chunks),
        compiler_params=PARAMS,
        cost_estimate=pl.CostEstimate(flops=10_000_000, bytes_accessed=8_000_000, transcendentals=0),
    )(info, parents, mine, theirs, *later_than)


def plus(*terms):
    return sum(term.astype(F32) for term in terms).astype(BF)


def scatter(info, parents, mine):
    theirs = shift(mine, "core", 1)
    sums = dict(zip(FIRST, combine(FIRST, info, parents, mine, theirs)))
    up = shift(sums[4], "z", 1)
    down = shift(sums[5], "z", -1)
    sums |= zip(REST, combine(REST, info, parents, mine, theirs, sums[4]))
    half = NX // 2
    up = jnp.concatenate([plus(sums[3][:half], up), sums[3][half:]])
    down = jnp.concatenate([sums[6][:half], plus(sums[6][half:], down)])
    for a, b in ((2, 7), (1, 8)):
        up = plus(sums[a], shift(up, "z", 1))
        down = plus(sums[b], shift(down, "z", -1))
    line = plus(sums[0], shift(up, "z", 1), shift(down, "z", -1))
    return (
        line[0].astype(F32)
        + shift(line[1], "x", 1).astype(F32)
        + shift(line[2], "x", 2).astype(F32)
        + shift(line[3], "x", -1).astype(F32)
    )


def body(queries, keys, values, grad_out, out_weight, parents, lengths):
    z = lax.axis_index("z")
    x = lax.axis_index("x")
    core = lax.axis_index("core")
    info = jnp.stack([z, x, core, lax.axis_index("mp"), (z * NX + x) * NC + core]).astype(jnp.int32)
    block = jnp.concatenate([keys[:SEG], values[:SEG]], axis=1)
    pieces, attn_grad = gather(info, lengths, block, grad_out, out_weight)
    near, other = pieces[:9], pieces[9:]
    attended, full, lse = attend_forward(
        info, parents, lengths, queries, keys, values, near, other
    )
    grad_queries, own, slots = attend_backward(
        info, parents, lengths, queries, attn_grad, keys, values, full, lse, near, other
    )
    remote = scatter(info, parents, slots)
    gradients = jnp.concatenate([own[:SEG] + remote, own[SEG:]])
    return (
        attended,
        grad_queries,
        gradients[:, :128].astype(BF),
        gradients[:, 128:].astype(BF),
    )


def solution(mesh):
    fine = Mesh(mesh.devices.reshape(NZ, NX, NC, 4), ("z", "x", "core", "mp"))
    rows = ("z", "x", "core")
    return jax.shard_map(
        body,
        mesh=fine,
        in_specs=(P(rows, "mp"),) * 4 + (P("mp", None), P(), P()),
        out_specs=(P(rows, "mp"),) * 4,
        check_vma=False,
    )
```

```python
import functools
import math

import jax
import jax.numpy as jnp
from jax import lax
from jax.experimental import pallas as pl
from jax.experimental.pallas import tpu as pltpu
from jax.sharding import Mesh, PartitionSpec as P

SEG = 256
HOPS = 7
ROWS = HOPS * SEG + 2 * SEG
NZ, NX, NC = 8, 4, 2
NEG = -1e30
BF = jnp.bfloat16
F32 = jnp.float32
ANY = pl.BlockSpec(memory_space=pl.ANY)
SMEM = pl.BlockSpec(memory_space=pltpu.SMEM)
VMEM = pl.BlockSpec(memory_space=pltpu.VMEM)


def vmem(mib):
    return pltpu.CompilerParams(vmem_limit_bytes=mib * 1024 * 1024)


def shift(array, axis, step):
    size = {"z": NZ, "x": NX, "core": NC, "mp": 4}[axis]
    return lax.ppermute(array, axis, [(i, (i + step) % size) for i in range(size)])


def dot(left, right):
    return jnp.dot(left, right, preferred_element_type=F32)


def dot_nt(left, right):
    return lax.dot_general(left, right, (((1,), (1,)), ((), ())), preferred_element_type=F32)


def project_kernel(info, lengths, own, after, before, low, high, weight, out, own_buf, w_buf, total, sems):
    width = own.shape[1]
    copies = []
    for step in (1, 3, 2, 0):
        column = pl.multiple_of(lax.rem(info[3] + step, 4) * width, 128)
        copy = pltpu.make_async_copy(weight.at[:, pl.ds(column, width)], w_buf.at[step], sems.at[step])
        copy.start()
        copies.append((step, copy))
    own_copy = pltpu.make_async_copy(own, own_buf, sems.at[4])
    own_copy.start()
    for step, copy in copies:
        copy.wait()
        if step == 0:
            own_copy.wait()
        for s in range(2):
            rows = slice(s * SEG, (s + 1) * SEG)
            if step == 2:
                piece = (low, high)[s][...]
            else:
                piece = {1: after, 3: before, 0: own_buf}[step][rows, :]
            part = dot_nt(piece, w_buf[step])
            if step == 1:
                total[rows, :] = part
            elif step != 0:
                total[rows, :] += part
            else:
                row = lax.broadcasted_iota(jnp.int32, part.shape, 0)
                live = row < lengths[2 * info[4] + s]
                out[rows, :] = jnp.where(live, total[rows, :] + part, 0.0).astype(BF)


def project(info, lengths, own, after, before, low, high, out_weight):
    rows, width = own.shape
    heads = out_weight.shape[0]
    return pl.pallas_call(
        project_kernel,
        out_shape=jax.ShapeDtypeStruct((rows, heads), BF),
        in_specs=[SMEM, SMEM, ANY, VMEM, VMEM, VMEM, VMEM, ANY],
        out_specs=VMEM,
        scratch_shapes=[
            pltpu.VMEM((rows, width), BF),
            pltpu.VMEM((4, heads, width), BF),
            pltpu.VMEM((rows, heads), F32),
            pltpu.SemaphoreType.DMA((5,)),
        ],
        compiler_params=vmem(50),
        cost_estimate=pl.CostEstimate(flops=8 * rows * heads * width, bytes_accessed=12_000_000, transcendentals=0),
    )(info, lengths, own, after, before, low, high, out_weight)


def cut_kernel(ahead, back, low, high):
    low[...] = ahead[...]
    high[...] = back[...]


def cut(ahead, back):
    shape = (ahead.shape[0] // 2,) + ahead.shape[1:]
    half = jax.ShapeDtypeStruct(shape, ahead.dtype)
    rest = (0,) * (len(shape) - 1)
    return pl.pallas_call(
        cut_kernel,
        grid=(1,),
        out_shape=(half, half),
        in_specs=[
            pl.BlockSpec(shape, lambda i: (0,) + rest),
            pl.BlockSpec(shape, lambda i: (1,) + rest),
        ],
        out_specs=(pl.BlockSpec(shape, lambda i: (0,) + rest),) * 2,
        compiler_params=vmem(8),
        cost_estimate=pl.CostEstimate(flops=0, bytes_accessed=1_000_000, transcendentals=0),
    )(ahead, back)


def first_block_kernel(keys, values, out):
    out[:, :128] = keys[...]
    out[:, 128:] = values[...]


def first_block(keys, values):
    block = pl.BlockSpec((SEG, 128), lambda i: (0, 0))
    return pl.pallas_call(
        first_block_kernel,
        grid=(1,),
        out_shape=jax.ShapeDtypeStruct((SEG, 256), keys.dtype),
        in_specs=[block, block],
        out_specs=pl.BlockSpec((SEG, 256), lambda i: (0, 0)),
        compiler_params=vmem(4),
    )(keys, values)


def gather(info, lengths, block, grad_out, out_weight):
    before = shift(grad_out, "mp", 1)
    after = shift(grad_out, "mp", -1)
    line = jnp.stack(
        [block, shift(block, "x", -1), shift(block, "x", 2), shift(block, "x", 1)]
    )
    ahead = [line]
    back = [line]
    for _ in range(3):
        ahead.append(shift(ahead[-1], "z", -1))
        back.append(shift(back[-1], "z", 1))
    low, high = cut(after, before)
    low = shift(low, "mp", -1)
    high = shift(high, "mp", 1)
    far_low, far_high = cut(ahead[3], back[3])
    far_low = shift(far_low, "z", -1)
    far_high = shift(far_high, "z", 1)
    pieces = [line, ahead[1], ahead[2], ahead[3], far_low, far_high, back[3], back[2], back[1]]
    pieces += [shift(piece, "core", 1) for piece in pieces]
    return pieces, project(info, lengths, grad_out, after, before, low, high, out_weight)


def for_piece(dz, dx, action):
    for k in range(4):
        pl.when(dz == k)(functools.partial(action, k, dx))
    pl.when((dz == 4) & (dx < 2))(functools.partial(action, 4, dx))
    pl.when((dz == 4) & (dx >= 2))(functools.partial(action, 5, dx - 2))
    for k in range(5, 8):
        pl.when(dz == k)(functools.partial(action, k + 1, dx))


def place(info, ancestor):
    owner = lax.div(ancestor, 2)
    dz = lax.rem(lax.div(owner, NX * NC) - info[0] + NZ, NZ)
    dx = lax.rem(lax.rem(lax.div(owner, NC), NX) - info[1] + NX, NX)
    return dz, dx, lax.rem(owner, NC) == info[2]


def start_fetch(info, parents, lengths, near, other, kv, lens, sems):
    depths = []
    for s in range(2):

        def hop(i, carry, s=s):
            current, depth = carry
            current = jnp.where(current >= 0, parents[jnp.maximum(current, 0)], -1)
            slot = s * HOPS + i

            @pl.when(current >= 0)
            def _():
                lens[slot] = lengths[current]
                dz, dx, same = place(info, current)

                def start(source, k, b):
                    pltpu.make_async_copy(source[k].at[b], kv.at[slot], sems.at[slot]).start()

                @pl.when(same)
                def _():
                    for_piece(dz, dx, functools.partial(start, near))

                @pl.when(jnp.logical_not(same))
                def _():
                    for_piece(dz, dx, functools.partial(start, other))

            return current, depth + (current >= 0).astype(jnp.int32)

        depths.append(lax.fori_loop(0, HOPS, hop, (2 * info[4] + s, jnp.int32(0)))[1])
    return depths


def wait_fetch(near, kv, sems, slot):
    pltpu.make_async_copy(near[0].at[0], kv.at[slot], sems.at[slot]).wait()


def pack(slot, depth, near, kv, lens, starts, sems, store):
    def one(i, row):
        wait_fetch(near, kv, sems, slot + i)
        starts[slot + i] = row
        store(row, kv[slot + i, :, :128], kv[slot + i, :, 128:], lens[slot + i])
        return row + (lens[slot + i] + 15) // 16 * 16

    total = lax.fori_loop(0, depth, one, jnp.int32(0))
    none = jnp.zeros((SEG, 128), BF)
    for i in range(2):
        store(total + i * SEG, none, none, 0)
    return total


def rows_at(row, count):
    return pl.ds(pl.multiple_of(row, 16), count)


def for_rows(total, step):
    def whole(i, _):
        step(512 * i, 512)
        return 0

    count = (total + 255) // 512
    lax.fori_loop(0, count, whole, 0)
    rest = total - 512 * count
    pl.when((rest > 0) & (rest <= 128))(lambda: step(512 * count, 128))
    pl.when(rest > 128)(lambda: step(512 * count, 256))


def widen(block, length):
    row = lax.broadcasted_iota(jnp.int32, block.shape, 0)
    col = lax.broadcasted_iota(jnp.int32, block.shape, 1)
    bias = jnp.where(row < length, 0.0, NEG)
    extra = jnp.where(col == 0, bias, jnp.where(col < 4, 1.0, 0.0))
    return jnp.concatenate([block, extra.astype(BF)], axis=1)


def split_rows(lead, value):
    high = value.astype(BF).astype(F32)
    mid = (value - high).astype(BF).astype(F32)
    low = value - high - mid
    shape = (128, value.shape[1])
    row = lax.broadcasted_iota(jnp.int32, shape, 0)
    out = jnp.where(row == 0, lead, 0.0)
    for i, part in enumerate((high, mid, low)):
        out = jnp.where(row == i + 1, jnp.broadcast_to(part, shape), out)
    return out.astype(BF)


def head_spans(width):
    return [slice(h * SEG, (h + 1) * SEG) for h in range(width // SEG)]


def own_mask(length):
    key_row = lax.broadcasted_iota(jnp.int32, (SEG, SEG), 0)
    query_row = lax.broadcasted_iota(jnp.int32, (SEG, SEG), 1)
    return (key_row <= query_row) & (key_row < length)


def forward_kernel(info, parents, lengths, q, ko, vo, *refs):
    near, other = refs[:9], refs[9:18]
    att_out, full_out, lse_out = refs[18:21]
    kv, k_rows, v_rows, q_t, m_ref, l_ref, lens, starts, sems = refs[21:]
    width = q_t.shape[1]
    coef = math.log2(math.e) / math.sqrt(128)
    first = 2 * info[4]
    spans = head_spans(width)
    depths = start_fetch(info, parents, lengths, near, other, kv, lens, sems)

    for s in range(2):
        rows = slice(s * SEG, (s + 1) * SEG)
        att = full_out.at[s]
        q_t[128:, :] = split_rows(1.0, jnp.zeros((1, width), F32))
        for h, span in enumerate(spans):
            q_t[:128, span] = q[rows, h * 128 : (h + 1) * 128].T

        def update(blocks, mask=None, s=s, att=att):
            v_t = jnp.concatenate([v.T for _, v in blocks], axis=1)
            scores = [[dot(k, q_t[:, span]) for k, _ in blocks] for span in spans]
            if mask is None:
                old = [m_ref[:, span] for span in spans]
                old_l = [l_ref[:, span] for span in spans]
            tops, probs, totals, scales = [], [], [], []
            for h, group in enumerate(scores):
                if mask is not None:
                    group = [jnp.where(mask, group[0], NEG)]
                top = functools.reduce(
                    jnp.maximum, [jnp.max(x, axis=0, keepdims=True) for x in group]
                )
                if mask is None:
                    top = jnp.maximum(top, old[h])
                    scales.append(jnp.exp2((old[h] - top) * coef))
                p = [jnp.exp2((x - top) * coef) for x in group]
                totals.append(sum(jnp.sum(x, axis=0, keepdims=True) for x in p))
                tops.append(top)
                probs.append(jnp.concatenate([x.astype(BF) for x in p], axis=0))
            parts = [dot(v_t, p) for p in probs]
            for h, span in enumerate(spans):
                m_ref[:, span] = tops[h]
                if mask is None:
                    l_ref[:, span] = old_l[h] * scales[h] + totals[h]
                    att[:, span] = att[:, span] * scales[h] + parts[h]
                else:
                    l_ref[:, span] = totals[h]
                    att[:, span] = parts[h]

        length = lengths[first + s]
        update([(widen(ko[rows, :], length), vo[rows, :])], own_mask(length))

        def store(row, k, v, used):
            k_rows[rows_at(row, SEG), :] = widen(k, used)
            v_rows[rows_at(row, SEG), :] = v

        def step(row, count, update=update):
            here = rows_at(row, count)
            update([(k_rows[here, :], v_rows[here, :])])

        for_rows(pack(s * HOPS, depths[s], near, kv, lens, starts, sems, store), step)
        for h, span in enumerate(spans):
            total = l_ref[:, span]
            full = att[:, span] * (1.0 / total)
            att[:, span] = full
            lse_out[s, :, span] = m_ref[:, span] + jnp.log2(total) * (1.0 / coef)
            att_out[rows, h * 128 : (h + 1) * 128] = full.T.astype(BF)


def backward_kernel(info, parents, lengths, q, do, ko, vo, full, lse, *refs):
    near, other = refs[:9], refs[9:18]
    dq_out, own_out, slots = refs[18:21]
    kv, k_rows, v_rows, dk_rows, dv_rows, q_t, q_st, do_t, do_st, dq_t, lens, starts, sems = refs[21:]
    width = q_t.shape[1]
    scale = 1.0 / math.sqrt(128)
    coef = math.log2(math.e) / math.sqrt(128)
    first = 2 * info[4]
    spans = head_spans(width)
    depths = start_fetch(info, parents, lengths, near, other, kv, lens, sems)

    for s in range(2):
        rows = slice(s * SEG, (s + 1) * SEG)
        for h, span in enumerate(spans):
            cols = slice(h * 128, (h + 1) * 128)
            q_st[span, :] = q[rows, cols]
            q_t[:128, span] = q[rows, cols].T
            do_st[span, :] = do[rows, cols]
            turned = do[rows, cols].T
            do_t[:128, span] = turned
            inner = jnp.sum(turned.astype(F32) * full[s, :, span], axis=0, keepdims=True)
            q_t[128:, span] = split_rows(1.0, -lse[s, :, span])
            do_t[128:, span] = split_rows(0.0, -inner)

        def update(blocks, mask=None):
            k_t = jnp.concatenate([k[:, :128].T for k, _ in blocks], axis=1)
            keys = [k for k, _ in blocks]
            vals = [v for _, v in blocks]
            scores = [[dot(k, q_t[:, span]) for k in keys] for span in spans]
            grads = [[dot(v, do_t[:, span]) for v in vals] for span in spans]
            probs = [[] for _ in blocks]
            steps = [[] for _ in blocks]
            for h in range(len(spans)):
                for j in range(len(blocks)):
                    x = scores[h][j]
                    if mask is not None:
                        x = jnp.where(mask, x, NEG)
                    p = jnp.exp2(x * coef)
                    probs[j].append(p.astype(BF))
                    steps[j].append((p * grads[h][j]).astype(BF))
            for h, span in enumerate(spans):
                part = dot(k_t, jnp.concatenate([d[h] for d in steps], axis=0))
                if mask is None:
                    dq_t[:, span] += part
                else:
                    dq_t[:, span] = part
            return [
                (
                    dot(jnp.concatenate(steps[j], axis=1), q_st[...]) * scale,
                    dot(jnp.concatenate(probs[j], axis=1), do_st[...]),
                )
                for j in range(len(blocks))
            ]

        length = lengths[first + s]
        ((dk, dv),) = update([(widen(ko[rows, :], length), widen(vo[rows, :], length))], own_mask(length))
        own_out[rows, :128] = dk
        own_out[rows, 128:] = dv

        def store(row, k, v, used):
            k_rows[rows_at(row, SEG), :] = widen(k, used)
            v_rows[rows_at(row, SEG), :] = widen(v, used)

        def step(row, count, update=update):
            here = rows_at(row, count)
            ((dk, dv),) = update([(k_rows[here, :], v_rows[here, :])])
            dk_rows[here, :] = dk.astype(BF)
            dv_rows[here, :] = dv.astype(BF)

        for_rows(pack(s * HOPS, depths[s], near, kv, lens, starts, sems, store), step)

        def unpack(i, _, s=s):
            slot = s * HOPS + i
            here = rows_at(starts[slot], SEG)
            used = lax.broadcasted_iota(jnp.int32, (SEG, 128), 0) < lens[slot]
            zero = jnp.zeros((SEG, 128), BF)
            slots[slot, :, :128] = jnp.where(used, dk_rows[here, :], zero)
            slots[slot, :, 128:] = jnp.where(used, dv_rows[here, :], zero)
            return 0

        lax.fori_loop(0, depths[s], unpack, 0)
        for h, span in enumerate(spans):
            dq_out[rows, h * 128 : (h + 1) * 128] = (dq_t[:, span] * scale).T.astype(BF)


def attend_forward(info, parents, lengths, q, ko, vo, near, other):
    rows, features = q.shape
    width = features // 128 * SEG
    return pl.pallas_call(
        forward_kernel,
        out_shape=(
            jax.ShapeDtypeStruct((rows, features), BF),
            jax.ShapeDtypeStruct((2, 128, width), F32),
            jax.ShapeDtypeStruct((2, 1, width), F32),
        ),
        in_specs=[SMEM, SMEM, SMEM, VMEM, VMEM, VMEM] + [ANY] * 18,
        out_specs=(VMEM,) * 3,
        scratch_shapes=[
            pltpu.VMEM((2 * HOPS, SEG, 256), BF),
            pltpu.VMEM((ROWS, 256), BF),
            pltpu.VMEM((ROWS, 128), BF),
            pltpu.VMEM((256, width), BF),
            pltpu.VMEM((1, width), F32),
            pltpu.VMEM((1, width), F32),
            pltpu.SMEM((2 * HOPS,), jnp.int32),
            pltpu.SMEM((2 * HOPS,), jnp.int32),
            pltpu.SemaphoreType.DMA((2 * HOPS,)),
        ],
        compiler_params=vmem(18),
        cost_estimate=pl.CostEstimate(flops=3_000_000_000, bytes_accessed=8_000_000, transcendentals=5_000_000),
    )(info, parents, lengths, q, ko, vo, *near, *other)


def attend_backward(info, parents, lengths, q, do, ko, vo, full, lse, near, other):
    rows, features = q.shape
    width = features // 128 * SEG
    return pl.pallas_call(
        backward_kernel,
        out_shape=(
            jax.ShapeDtypeStruct((rows, features), BF),
            jax.ShapeDtypeStruct((rows, 256), F32),
            jax.ShapeDtypeStruct((2 * HOPS, SEG, 256), BF),
        ),
        in_specs=[SMEM, SMEM, SMEM] + [VMEM] * 6 + [ANY] * 18,
        out_specs=(VMEM,) * 3,
        scratch_shapes=[
            pltpu.VMEM((2 * HOPS, SEG, 256), BF),
            pltpu.VMEM((ROWS, 256), BF),
            pltpu.VMEM((ROWS, 256), BF),
            pltpu.VMEM((ROWS, 128), BF),
            pltpu.VMEM((ROWS, 128), BF),
            pltpu.VMEM((256, width), BF),
            pltpu.VMEM((width, 128), BF),
            pltpu.VMEM((256, width), BF),
            pltpu.VMEM((width, 128), BF),
            pltpu.VMEM((128, width), F32),
            pltpu.SMEM((2 * HOPS,), jnp.int32),
            pltpu.SMEM((2 * HOPS,), jnp.int32),
            pltpu.SemaphoreType.DMA((2 * HOPS,)),
        ],
        compiler_params=vmem(26),
        cost_estimate=pl.CostEstimate(flops=8_000_000_000, bytes_accessed=8_000_000, transcendentals=5_000_000),
    )(info, parents, lengths, q, do, ko, vo, full, lse, *near, *other)


FIRST = ((0, 4), (1, 4), (0, 5), (1, 3))
REST = tuple((half, dz) for half in range(2) for dz in range(NZ) if (half, dz) not in FIRST)


def combine_kernel(chunks, info, parents, mine, theirs, *refs):
    outs = refs[-len(chunks) :]
    for out in outs:
        out[...] = jnp.zeros(out.shape, BF)
    for source, device in ((mine, info[4]), (theirs, info[4] + 1 - 2 * info[2])):
        for s in range(2):

            def hop(i, current, source=source, device=device, s=s):
                current = jnp.where(current >= 0, parents[jnp.maximum(current, 0)], -1)
                dz, dx, same = place(info, current)

                @pl.when((current >= 0) & same)
                def _():
                    for (half, k), out in zip(chunks, outs):

                        @pl.when(dz == k)
                        def _(half=half, out=out):
                            term = source[s * HOPS + i, :, half * 128 : half * 128 + 128]
                            out[dx] = (out[dx].astype(F32) + term.astype(F32)).astype(BF)

                return current

            lax.fori_loop(0, HOPS, hop, 2 * device + s)


def combine(chunks, info, parents, mine, theirs, *later_than):
    return pl.pallas_call(
        functools.partial(combine_kernel, chunks),
        out_shape=tuple(jax.ShapeDtypeStruct((NX, SEG, 128), BF) for _ in chunks),
        in_specs=[SMEM, SMEM, VMEM, VMEM] + [ANY] * len(later_than),
        out_specs=(VMEM,) * len(chunks),
        compiler_params=vmem(8),
        cost_estimate=pl.CostEstimate(flops=10_000_000, bytes_accessed=8_000_000, transcendentals=0),
    )(info, parents, mine, theirs, *later_than)


def plus(*terms):
    return sum(term.astype(F32) for term in terms).astype(BF)


def scatter(info, parents, mine):
    theirs = shift(mine, "core", 1)
    chunk = dict(zip(FIRST, combine(FIRST, info, parents, mine, theirs)))
    chunk |= zip(REST, combine(REST, info, parents, mine, theirs, chunk[FIRST[0]]))

    def chain(half, distances, step):
        total = chunk[half, distances[0]]
        for distance in distances[1:]:
            total = plus(chunk[half, distance], shift(total, "z", step))
        return shift(total, "z", step)

    up = chain(0, (4, 3, 2, 1), 1), chain(1, (3, 2, 1), 1)
    down = chain(0, (5, 6, 7), -1), chain(1, (4, 5, 6, 7), -1)
    line = jnp.concatenate([plus(chunk[h, 0], up[h], down[h]) for h in range(2)], axis=2)
    return (
        line[0].astype(F32)
        + shift(line[1], "x", 1).astype(F32)
        + shift(line[2], "x", 2).astype(F32)
        + shift(line[3], "x", -1).astype(F32)
    )


def body(queries, keys, values, grad_out, out_weight, parents, lengths):
    z = lax.axis_index("z")
    x = lax.axis_index("x")
    core = lax.axis_index("core")
    info = jnp.stack([z, x, core, lax.axis_index("mp"), (z * NX + x) * NC + core]).astype(jnp.int32)
    block = first_block(keys, values)
    pieces, attn_grad = gather(info, lengths, block, grad_out, out_weight)
    near, other = pieces[:9], pieces[9:]
    attended, full, lse = attend_forward(
        info, parents, lengths, queries, keys, values, near, other
    )
    grad_queries, own, slots = attend_backward(
        info, parents, lengths, queries, attn_grad, keys, values, full, lse, near, other
    )
    remote = scatter(info, parents, slots)
    gradients = jnp.concatenate([own[:SEG] + remote, own[SEG:]])
    return (
        attended,
        grad_queries,
        gradients[:, :128].astype(BF),
        gradients[:, 128:].astype(BF),
    )


def solution(mesh):
    fine = Mesh(mesh.devices.reshape(NZ, NX, NC, 4), ("z", "x", "core", "mp"))
    rows = ("z", "x", "core")
    return jax.shard_map(
        body,
        mesh=fine,
        in_specs=(P(rows, "mp"),) * 4 + (P("mp", None), P(), P()),
        out_specs=(P(rows, "mp"),) * 4,
        check_vma=False,
    )
```

```python
import functools
import math

import jax
import jax.numpy as jnp
from jax import lax
from jax.experimental import pallas as pl
from jax.experimental.pallas import tpu as pltpu
from jax.sharding import Mesh, PartitionSpec as P

SEG = 256
HOPS = 7
ROWS = HOPS * SEG + 2 * SEG
NZ, NX, NC = 8, 4, 2
NEG = -1e30
BF = jnp.bfloat16
F32 = jnp.float32
ANY = pl.BlockSpec(memory_space=pl.ANY)
SMEM = pl.BlockSpec(memory_space=pltpu.SMEM)
VMEM = pl.BlockSpec(memory_space=pltpu.VMEM)


def vmem(mib):
    return pltpu.CompilerParams(vmem_limit_bytes=mib * 1024 * 1024)


def shift(array, axis, step):
    size = {"z": NZ, "x": NX, "core": NC, "mp": 4}[axis]
    return lax.ppermute(array, axis, [(i, (i + step) % size) for i in range(size)])


def dot(left, right):
    return jnp.dot(left, right, preferred_element_type=F32)


def dot_nt(left, right):
    return lax.dot_general(left, right, (((1,), (1,)), ((), ())), preferred_element_type=F32)


def project_kernel(info, lengths, own, after, before, low, high, weight, out, own_buf, w_buf, total, sems):
    width = own.shape[1]
    copies = []
    for step in (1, 3, 2, 0):
        column = pl.multiple_of(lax.rem(info[3] + step, 4) * width, 128)
        copy = pltpu.make_async_copy(weight.at[:, pl.ds(column, width)], w_buf.at[step], sems.at[step])
        copy.start()
        copies.append((step, copy))
    own_copy = pltpu.make_async_copy(own, own_buf, sems.at[4])
    own_copy.start()
    for step, copy in copies:
        copy.wait()
        if step == 0:
            own_copy.wait()
        for s in range(2):
            rows = slice(s * SEG, (s + 1) * SEG)
            if step == 2:
                piece = (low, high)[s][...]
            else:
                piece = {1: after, 3: before, 0: own_buf}[step][rows, :]
            part = dot_nt(piece, w_buf[step])
            if step == 1:
                total[rows, :] = part
            elif step != 0:
                total[rows, :] += part
            else:
                row = lax.broadcasted_iota(jnp.int32, part.shape, 0)
                live = row < lengths[2 * info[4] + s]
                out[rows, :] = jnp.where(live, total[rows, :] + part, 0.0).astype(BF)


def project(info, lengths, own, after, before, low, high, out_weight):
    rows, width = own.shape
    heads = out_weight.shape[0]
    return pl.pallas_call(
        project_kernel,
        out_shape=jax.ShapeDtypeStruct((rows, heads), BF),
        in_specs=[SMEM, SMEM, ANY, VMEM, VMEM, VMEM, VMEM, ANY],
        out_specs=VMEM,
        scratch_shapes=[
            pltpu.VMEM((rows, width), BF),
            pltpu.VMEM((4, heads, width), BF),
            pltpu.VMEM((rows, heads), F32),
            pltpu.SemaphoreType.DMA((5,)),
        ],
        compiler_params=vmem(43),
        cost_estimate=pl.CostEstimate(flops=8 * rows * heads * width, bytes_accessed=12_000_000, transcendentals=0),
    )(info, lengths, own, after, before, low, high, out_weight)


def cut_kernel(ahead, back, low, high):
    low[...] = ahead[...]
    high[...] = back[...]


def cut(ahead, back):
    shape = (ahead.shape[0] // 2,) + ahead.shape[1:]
    half = jax.ShapeDtypeStruct(shape, ahead.dtype)
    rest = (0,) * (len(shape) - 1)
    return pl.pallas_call(
        cut_kernel,
        grid=(1,),
        out_shape=(half, half),
        in_specs=[
            pl.BlockSpec(shape, lambda i: (0,) + rest),
            pl.BlockSpec(shape, lambda i: (1,) + rest),
        ],
        out_specs=(pl.BlockSpec(shape, lambda i: (0,) + rest),) * 2,
        compiler_params=vmem(8),
        cost_estimate=pl.CostEstimate(flops=0, bytes_accessed=1_000_000, transcendentals=0),
    )(ahead, back)


def first_block_kernel(keys, values, out):
    out[:, :128] = keys[...]
    out[:, 128:] = values[...]


def first_block(keys, values):
    block = pl.BlockSpec((SEG, 128), lambda i: (0, 0))
    return pl.pallas_call(
        first_block_kernel,
        grid=(1,),
        out_shape=jax.ShapeDtypeStruct((SEG, 256), keys.dtype),
        in_specs=[block, block],
        out_specs=pl.BlockSpec((SEG, 256), lambda i: (0, 0)),
        compiler_params=vmem(4),
    )(keys, values)


def gather(info, lengths, block, grad_out, out_weight):
    before = shift(grad_out, "mp", 1)
    after = shift(grad_out, "mp", -1)
    line = jnp.stack(
        [block, shift(block, "x", -1), shift(block, "x", 2), shift(block, "x", 1)]
    )
    ahead = [line]
    back = [line]
    for _ in range(3):
        ahead.append(shift(ahead[-1], "z", -1))
        back.append(shift(back[-1], "z", 1))
    low, high = cut(after, before)
    low = shift(low, "mp", -1)
    high = shift(high, "mp", 1)
    far_low, far_high = cut(ahead[3], back[3])
    far_low = shift(far_low, "z", -1)
    far_high = shift(far_high, "z", 1)
    pieces = [line, ahead[1], ahead[2], ahead[3], far_low, far_high, back[3], back[2], back[1]]
    pieces += [shift(piece, "core", 1) for piece in pieces]
    return pieces, project(info, lengths, grad_out, after, before, low, high, out_weight)


def for_piece(dz, dx, action):
    @pl.when(dz < 4)
    def _():
        for k in range(4):
            pl.when(dz == k)(functools.partial(action, k, dx))

    @pl.when(dz >= 4)
    def _():
        pl.when((dz == 4) & (dx < 2))(functools.partial(action, 4, dx))
        pl.when((dz == 4) & (dx >= 2))(functools.partial(action, 5, dx - 2))
        for k in range(5, 8):
            pl.when(dz == k)(functools.partial(action, k + 1, dx))


def place(info, ancestor):
    owner = lax.div(ancestor, 2)
    dz = lax.rem(lax.div(owner, NX * NC) - info[0] + NZ, NZ)
    dx = lax.rem(lax.rem(lax.div(owner, NC), NX) - info[1] + NX, NX)
    return dz, dx, lax.rem(owner, NC) == info[2]


def start_fetch(info, parents, lengths, near, other, kv, lens, sems):
    depths = []
    for s in range(2):

        def hop(i, carry, s=s):
            current, depth = carry
            current = jnp.where(current >= 0, parents[jnp.maximum(current, 0)], -1)
            slot = s * HOPS + i

            @pl.when(current >= 0)
            def _():
                lens[slot] = lengths[current]
                dz, dx, same = place(info, current)

                def start(source, k, b):
                    pltpu.make_async_copy(source[k].at[b], kv.at[slot], sems.at[slot]).start()

                @pl.when(same)
                def _():
                    for_piece(dz, dx, functools.partial(start, near))

                @pl.when(jnp.logical_not(same))
                def _():
                    for_piece(dz, dx, functools.partial(start, other))

            return current, depth + (current >= 0).astype(jnp.int32)

        depths.append(lax.fori_loop(0, HOPS, hop, (2 * info[4] + s, jnp.int32(0)))[1])
    return depths


def wait_fetch(near, kv, sems, slot):
    pltpu.make_async_copy(near[0].at[0], kv.at[slot], sems.at[slot]).wait()


def pack(slot, depth, near, kv, lens, starts, sems, store):
    def one(i, row):
        wait_fetch(near, kv, sems, slot + i)
        starts[slot + i] = row
        store(row, kv[slot + i, :, :128], kv[slot + i, :, 128:], lens[slot + i])
        return row + (lens[slot + i] + 15) // 16 * 16

    total = lax.fori_loop(0, depth, one, jnp.int32(0))
    none = jnp.zeros((SEG, 128), BF)
    for i in range(2):
        store(total + i * SEG, none, none, 0)
    return total


def rows_at(row, count):
    return pl.ds(pl.multiple_of(row, 16), count)


def for_rows(total, step):
    def whole(i, _):
        step(512 * i, 512)
        return 0

    count = (total + 255) // 512
    lax.fori_loop(0, count, whole, 0)
    rest = total - 512 * count
    pl.when((rest > 0) & (rest <= 128))(lambda: step(512 * count, 128))
    pl.when(rest > 128)(lambda: step(512 * count, 256))


def widen(block, length):
    row = lax.broadcasted_iota(jnp.int32, block.shape, 0)
    col = lax.broadcasted_iota(jnp.int32, block.shape, 1)
    bias = jnp.where(row < length, 0.0, NEG)
    extra = jnp.where(col == 0, bias, jnp.where(col < 4, 1.0, 0.0))
    return jnp.concatenate([block, extra.astype(BF)], axis=1)


def split_rows(lead, value):
    high = value.astype(BF).astype(F32)
    mid = (value - high).astype(BF).astype(F32)
    low = value - high - mid
    shape = (128, value.shape[1])
    row = lax.broadcasted_iota(jnp.int32, shape, 0)
    out = jnp.where(row == 0, lead, 0.0)
    for i, part in enumerate((high, mid, low)):
        out = jnp.where(row == i + 1, jnp.broadcast_to(part, shape), out)
    return out.astype(BF)


def head_spans(width):
    return [slice(h * SEG, (h + 1) * SEG) for h in range(width // SEG)]


def own_mask(length):
    key_row = lax.broadcasted_iota(jnp.int32, (SEG, SEG), 0)
    query_row = lax.broadcasted_iota(jnp.int32, (SEG, SEG), 1)
    return (key_row <= query_row) & (key_row < length)


def forward_kernel(info, parents, lengths, q, ko, vo, *refs):
    near, other = refs[:9], refs[9:18]
    att_out, full_out, lse_out = refs[18:21]
    kv, k_rows, v_rows, q_t, m_ref, l_ref, lens, starts, sems = refs[21:]
    width = q_t.shape[1]
    coef = math.log2(math.e) / math.sqrt(128)
    first = 2 * info[4]
    spans = head_spans(width)
    depths = start_fetch(info, parents, lengths, near, other, kv, lens, sems)

    for s in range(2):
        rows = slice(s * SEG, (s + 1) * SEG)
        att = full_out.at[s]
        q_t[128:, :] = split_rows(1.0, jnp.zeros((1, width), F32))
        for h, span in enumerate(spans):
            q_t[:128, span] = q[rows, h * 128 : (h + 1) * 128].T

        def update(blocks, mask=None, s=s, att=att):
            v_t = jnp.concatenate([v.T for _, v in blocks], axis=1)
            scores = [[dot(k, q_t[:, span]) for k, _ in blocks] for span in spans]
            if mask is None:
                old = [m_ref[:, span] for span in spans]
                old_l = [l_ref[:, span] for span in spans]
            tops, probs, totals, scales = [], [], [], []
            for h, group in enumerate(scores):
                if mask is not None:
                    group = [jnp.where(mask, group[0], NEG)]
                top = functools.reduce(
                    jnp.maximum, [jnp.max(x, axis=0, keepdims=True) for x in group]
                )
                if mask is None:
                    top = jnp.maximum(top, old[h])
                    scales.append(jnp.exp2((old[h] - top) * coef))
                p = [jnp.exp2((x - top) * coef) for x in group]
                totals.append(sum(jnp.sum(x, axis=0, keepdims=True) for x in p))
                tops.append(top)
                probs.append(jnp.concatenate([x.astype(BF) for x in p], axis=0))
            parts = [dot(v_t, p) for p in probs]
            for h, span in enumerate(spans):
                m_ref[:, span] = tops[h]
                if mask is None:
                    l_ref[:, span] = old_l[h] * scales[h] + totals[h]
                    att[:, span] = att[:, span] * scales[h] + parts[h]
                else:
                    l_ref[:, span] = totals[h]
                    att[:, span] = parts[h]

        length = lengths[first + s]
        update([(widen(ko[rows, :], length), vo[rows, :])], own_mask(length))

        def store(row, k, v, used):
            k_rows[rows_at(row, SEG), :] = widen(k, used)
            v_rows[rows_at(row, SEG), :] = v

        def step(row, count, update=update):
            here = rows_at(row, count)
            update([(k_rows[here, :], v_rows[here, :])])

        for_rows(pack(s * HOPS, depths[s], near, kv, lens, starts, sems, store), step)
        for h, span in enumerate(spans):
            total = l_ref[:, span]
            full = att[:, span] * (1.0 / total)
            att[:, span] = full
            lse_out[s, :, span] = m_ref[:, span] + jnp.log2(total) * (1.0 / coef)
            att_out[rows, h * 128 : (h + 1) * 128] = full.T.astype(BF)


def backward_kernel(info, parents, lengths, q, do, ko, vo, full, lse, *refs):
    near, other = refs[:9], refs[9:18]
    dq_out, own_out, slots = refs[18:21]
    kv, k_rows, v_rows, dk_rows, dv_rows, q_t, q_st, do_t, do_st, dq_t, lens, starts, sems = refs[21:]
    width = q_t.shape[1]
    scale = 1.0 / math.sqrt(128)
    coef = math.log2(math.e) / math.sqrt(128)
    first = 2 * info[4]
    spans = head_spans(width)
    depths = start_fetch(info, parents, lengths, near, other, kv, lens, sems)

    for s in range(2):
        rows = slice(s * SEG, (s + 1) * SEG)
        for h, span in enumerate(spans):
            cols = slice(h * 128, (h + 1) * 128)
            q_st[span, :] = q[rows, cols]
            q_t[:128, span] = q[rows, cols].T
            do_st[span, :] = do[rows, cols]
            turned = do[rows, cols].T
            do_t[:128, span] = turned
            inner = jnp.sum(turned.astype(F32) * full[s, :, span], axis=0, keepdims=True)
            q_t[128:, span] = split_rows(1.0, -lse[s, :, span])
            do_t[128:, span] = split_rows(0.0, -inner)

        def update(blocks, mask=None):
            k_t = jnp.concatenate([k[:, :128].T for k, _ in blocks], axis=1)
            keys = [k for k, _ in blocks]
            vals = [v for _, v in blocks]
            scores = [[dot(k, q_t[:, span]) for k in keys] for span in spans]
            grads = [[dot(v, do_t[:, span]) for v in vals] for span in spans]
            probs = [[] for _ in blocks]
            steps = [[] for _ in blocks]
            for h in range(len(spans)):
                for j in range(len(blocks)):
                    x = scores[h][j]
                    if mask is not None:
                        x = jnp.where(mask, x, NEG)
                    p = jnp.exp2(x * coef)
                    probs[j].append(p.astype(BF))
                    steps[j].append((p * grads[h][j]).astype(BF))
            for h, span in enumerate(spans):
                part = dot(k_t, jnp.concatenate([d[h] for d in steps], axis=0))
                if mask is None:
                    dq_t[:, span] += part
                else:
                    dq_t[:, span] = part
            return [
                (
                    dot(jnp.concatenate(steps[j], axis=1), q_st[...]) * scale,
                    dot(jnp.concatenate(probs[j], axis=1), do_st[...]),
                )
                for j in range(len(blocks))
            ]

        length = lengths[first + s]
        ((dk, dv),) = update([(widen(ko[rows, :], length), widen(vo[rows, :], length))], own_mask(length))
        own_out[rows, :128] = dk
        own_out[rows, 128:] = dv

        def store(row, k, v, used):
            k_rows[rows_at(row, SEG), :] = widen(k, used)
            v_rows[rows_at(row, SEG), :] = widen(v, used)

        def step(row, count, update=update):
            here = rows_at(row, count)
            ((dk, dv),) = update([(k_rows[here, :], v_rows[here, :])])
            dk_rows[here, :] = dk.astype(BF)
            dv_rows[here, :] = dv.astype(BF)

        for_rows(pack(s * HOPS, depths[s], near, kv, lens, starts, sems, store), step)

        def unpack(i, _, s=s):
            slot = s * HOPS + i
            here = rows_at(starts[slot], SEG)
            used = lax.broadcasted_iota(jnp.int32, (SEG, 128), 0) < lens[slot]
            zero = jnp.zeros((SEG, 128), BF)
            slots[slot, :, :128] = jnp.where(used, dk_rows[here, :], zero)
            slots[slot, :, 128:] = jnp.where(used, dv_rows[here, :], zero)
            return 0

        lax.fori_loop(0, depths[s], unpack, 0)
        for h, span in enumerate(spans):
            dq_out[rows, h * 128 : (h + 1) * 128] = (dq_t[:, span] * scale).T.astype(BF)


def attend_forward(info, parents, lengths, q, ko, vo, near, other):
    rows, features = q.shape
    width = features // 128 * SEG
    return pl.pallas_call(
        forward_kernel,
        out_shape=(
            jax.ShapeDtypeStruct((rows, features), BF),
            jax.ShapeDtypeStruct((2, 128, width), F32),
            jax.ShapeDtypeStruct((2, 1, width), F32),
        ),
        in_specs=[SMEM, SMEM, SMEM, VMEM, VMEM, VMEM] + [ANY] * 18,
        out_specs=(VMEM,) * 3,
        scratch_shapes=[
            pltpu.VMEM((2 * HOPS, SEG, 256), BF),
            pltpu.VMEM((ROWS, 256), BF),
            pltpu.VMEM((ROWS, 128), BF),
            pltpu.VMEM((256, width), BF),
            pltpu.VMEM((1, width), F32),
            pltpu.VMEM((1, width), F32),
            pltpu.SMEM((2 * HOPS,), jnp.int32),
            pltpu.SMEM((2 * HOPS,), jnp.int32),
            pltpu.SemaphoreType.DMA((2 * HOPS,)),
        ],
        compiler_params=vmem(18),
        cost_estimate=pl.CostEstimate(flops=3_000_000_000, bytes_accessed=8_000_000, transcendentals=5_000_000),
    )(info, parents, lengths, q, ko, vo, *near, *other)


def attend_backward(info, parents, lengths, q, do, ko, vo, full, lse, near, other):
    rows, features = q.shape
    width = features // 128 * SEG
    return pl.pallas_call(
        backward_kernel,
        out_shape=(
            jax.ShapeDtypeStruct((rows, features), BF),
            jax.ShapeDtypeStruct((rows, 256), F32),
            jax.ShapeDtypeStruct((2 * HOPS, SEG, 256), BF),
        ),
        in_specs=[SMEM, SMEM, SMEM] + [VMEM] * 6 + [ANY] * 18,
        out_specs=(VMEM,) * 3,
        scratch_shapes=[
            pltpu.VMEM((2 * HOPS, SEG, 256), BF),
            pltpu.VMEM((ROWS, 256), BF),
            pltpu.VMEM((ROWS, 256), BF),
            pltpu.VMEM((ROWS, 128), BF),
            pltpu.VMEM((ROWS, 128), BF),
            pltpu.VMEM((256, width), BF),
            pltpu.VMEM((width, 128), BF),
            pltpu.VMEM((256, width), BF),
            pltpu.VMEM((width, 128), BF),
            pltpu.VMEM((128, width), F32),
            pltpu.SMEM((2 * HOPS,), jnp.int32),
            pltpu.SMEM((2 * HOPS,), jnp.int32),
            pltpu.SemaphoreType.DMA((2 * HOPS,)),
        ],
        compiler_params=vmem(26),
        cost_estimate=pl.CostEstimate(flops=8_000_000_000, bytes_accessed=8_000_000, transcendentals=5_000_000),
    )(info, parents, lengths, q, do, ko, vo, full, lse, *near, *other)


FIRST = ((0, 4), (1, 4), (0, 5), (1, 3))
REST = tuple((half, dz) for half in range(2) for dz in range(NZ) if (half, dz) not in FIRST)


def combine_kernel(chunks, info, parents, mine, theirs, *refs):
    outs = refs[-len(chunks) :]
    for out in outs:
        out[...] = jnp.zeros(out.shape, BF)
    for source, device in ((mine, info[4]), (theirs, info[4] + 1 - 2 * info[2])):
        for s in range(2):

            def hop(i, current, source=source, device=device, s=s):
                current = jnp.where(current >= 0, parents[jnp.maximum(current, 0)], -1)
                dz, dx, same = place(info, current)

                @pl.when((current >= 0) & same)
                def _():
                    for (half, k), out in zip(chunks, outs):

                        @pl.when(dz == k)
                        def _(half=half, out=out):
                            term = source[s * HOPS + i, :, half * 128 : half * 128 + 128]
                            out[dx] = (out[dx].astype(F32) + term.astype(F32)).astype(BF)

                return current

            lax.fori_loop(0, HOPS, hop, 2 * device + s)


def combine(chunks, info, parents, mine, theirs, *later_than):
    return pl.pallas_call(
        functools.partial(combine_kernel, chunks),
        out_shape=tuple(jax.ShapeDtypeStruct((NX, SEG, 128), BF) for _ in chunks),
        in_specs=[SMEM, SMEM, VMEM, VMEM] + [ANY] * len(later_than),
        out_specs=(VMEM,) * len(chunks),
        compiler_params=vmem(8),
        cost_estimate=pl.CostEstimate(flops=10_000_000, bytes_accessed=8_000_000, transcendentals=0),
    )(info, parents, mine, theirs, *later_than)


def plus(*terms):
    return sum(term.astype(F32) for term in terms).astype(BF)


def scatter(info, parents, mine):
    theirs = shift(mine, "core", 1)
    chunk = dict(zip(FIRST, combine(FIRST, info, parents, mine, theirs)))
    chunk |= zip(REST, combine(REST, info, parents, mine, theirs, chunk[FIRST[0]]))

    def chain(half, distances, step):
        total = chunk[half, distances[0]]
        for distance in distances[1:]:
            total = plus(chunk[half, distance], shift(total, "z", step))
        return shift(total, "z", step)

    up = chain(0, (4, 3, 2, 1), 1), chain(1, (3, 2, 1), 1)
    down = chain(0, (5, 6, 7), -1), chain(1, (4, 5, 6, 7), -1)
    line = jnp.concatenate([plus(chunk[h, 0], up[h], down[h]) for h in range(2)], axis=2)
    return (
        line[0].astype(F32)
        + shift(line[1], "x", 1).astype(F32)
        + shift(line[2], "x", 2).astype(F32)
        + shift(line[3], "x", -1).astype(F32)
    )


def body(queries, keys, values, grad_out, out_weight, parents, lengths):
    z = lax.axis_index("z")
    x = lax.axis_index("x")
    core = lax.axis_index("core")
    info = jnp.stack([z, x, core, lax.axis_index("mp"), (z * NX + x) * NC + core]).astype(jnp.int32)
    block = first_block(keys, values)
    pieces, attn_grad = gather(info, lengths, block, grad_out, out_weight)
    near, other = pieces[:9], pieces[9:]
    attended, full, lse = attend_forward(
        info, parents, lengths, queries, keys, values, near, other
    )
    grad_queries, own, slots = attend_backward(
        info, parents, lengths, queries, attn_grad, keys, values, full, lse, near, other
    )
    remote = scatter(info, parents, slots)
    gradients = jnp.concatenate([own[:SEG] + remote, own[SEG:]])
    return (
        attended,
        grad_queries,
        gradients[:, :128].astype(BF),
        gradients[:, 128:].astype(BF),
    )


def solution(mesh):
    fine = Mesh(mesh.devices.reshape(NZ, NX, NC, 4), ("z", "x", "core", "mp"))
    rows = ("z", "x", "core")
    return jax.shard_map(
        body,
        mesh=fine,
        in_specs=(P(rows, "mp"),) * 4 + (P("mp", None), P(), P()),
        out_specs=(P(rows, "mp"),) * 4,
        check_vma=False,
    )
```
